32 devices in a mesh: group: 2 (over y), row: 4 (over x, core), head: 4 (over z).
Axes of the slice: x: 2, y: 2, z: 4, core: 2. Of those that a mesh axis runs over, the one named last changes fastest.
Arguments:
- latent: bfloat16 [1024, 3072], P('row', 'head'), may hold values from -6 to 6
- hint: bfloat16 [1024, 3072], P('row', 'head'), may hold values from -6 to 6
- timestep: int32 [1], replicated, may hold values from 0 to 7
- modulation: float32 [2, 8, 3, 3072], P('group'), may hold values from -3 to 3
- qkv_weight: bfloat16 [2, 3, 3072, 3072], P('group', None, None, 'head'), may hold values from -0.109375 to 0.109375
- out_weight: bfloat16 [2, 3072, 3072], P('group', None, 'head'), may hold values from -0.109375 to 0.109375
- zero_weight: bfloat16 [3072, 3072], P(None, 'head'), may hold values from -0.109375 to 0.109375
- cotangent: bfloat16 [1024, 3072], P('row', 'head'), may hold values from -6 to 6
Outputs:
- mixed: bfloat16 [1024, 3072], P('row', 'head')
- latent_grad: float32 [4, 2, 128, 3072], P('row', 'group', None, 'head')
- hint_grad: float32 [4, 2, 128, 3072], P('row', 'group', None, 'head')
- qkv_grad: float32 [3072, 3, 3072], P(('group', 'row'), None, 'head')
- out_grad: float32 [3072, 3072], P(('group', 'row'), 'head')
- zero_grad: float32 [3072, 3072], P(('group', 'row'), 'head')
The draws below stay inside these ranges and needn't reach their ends.
All inputs are finite; a program needn't handle non-finite values.
Results may differ from the reference program's by a relative error of at most 0.015.
Values may be sent and summed in bfloat16 or wider, within the bound.
A program may use at most 128 MiB of HBM per device.

```python
import jax
import jax.numpy as jnp
from jax import lax

D = 3072
HEADS = 24
HD = 128
TOK_DEV = 256
STEPS = 8
TOKENS = 1024
N_ROW = 4


def block_scale(stream_key, dims, shards, low, top_value):
    gain = 1.0
    for dim, shards_of in shards:
        heights = jax.random.uniform(jax.random.fold_in(jax.random.fold_in(stream_key, 6), dim), (shards_of,), jnp.float32, low / len(shards), top_value / len(shards))
        gain = gain * jnp.repeat(jnp.exp(heights), dims[dim] // shards_of).reshape((-1,) + (1,) * (len(dims) - 1 - dim))
    return gain


def gaussian(key, shape, scale, limit, shards=(), held_as=jnp.bfloat16):
    drawn = scale * jax.random.normal(key, shape, jnp.float32)
    if shards:
        drawn = drawn * block_scale(key, shape, shards, -0.22, 0.18)
    return jnp.clip(drawn, -limit, limit).astype(held_as)


def setup_inputs(seed: int = 0) -> dict:
    key_list = jax.random.split(jax.random.key(seed), 9)
    latent = gaussian(key_list[0], (TOKENS, D), 1.0, 6.0, ((0, 4), (1, 4)))
    hint = gaussian(key_list[1], (TOKENS, D), 1.0, 6.0, ((0, 4), (1, 4)))
    timestep = jax.random.randint(key_list[2], (1,), 0, STEPS).astype(jnp.int32)
    modulation = gaussian(key_list[3], (2, STEPS, 3, D), 0.5, 3.0, ((0, 2),), jnp.float32)
    qkv_weight = gaussian(key_list[4], (2, 3, D, D), D ** -0.5, 0.109375, ((0, 2), (3, 4)))
    out_weight = gaussian(key_list[5], (2, D, D), D ** -0.5, 0.109375, ((0, 2), (2, 4)))
    zero_weight = gaussian(key_list[6], (D, D), D ** -0.5, 0.109375, ((1, 4),))
    cotangent = gaussian(key_list[7], (TOKENS, D), 1.0, 6.0, ((0, 4), (1, 4)))
    return dict(latent=latent, hint=hint, timestep=timestep, modulation=modulation, qkv_weight=qkv_weight, out_weight=out_weight, zero_weight=zero_weight, cotangent=cotangent)


EPS = 1e-06

def normalize(u, shift, scale):
    uf = u.astype(jnp.float32)
    mean = lax.optimization_barrier(jnp.mean(uf, axis=-1, keepdims=True))
    centred = uf - mean
    var = lax.optimization_barrier(jnp.mean(centred * centred, axis=-1, keepdims=True))
    rstd = lax.rsqrt(var + EPS)
    nhat = centred * rstd
    normed = (nhat * (1.0 + scale) + shift).astype(jnp.bfloat16)
    return (normed, nhat, rstd)

def split_heads(x):
    return x.reshape(TOKENS, HEADS, HD).transpose(1, 0, 2)

def merge_heads(x):
    return x.transpose(1, 0, 2).reshape(TOKENS, HEADS * HD)

def head_forward(args):
    qh, kh, vh = args
    scores = jnp.dot(qh, kh.T, preferred_element_type=jnp.float32) * HD ** (-0.5)
    top = lax.optimization_barrier(jnp.max(scores, axis=-1, keepdims=True))
    weights = jnp.exp(scores - top)
    total = lax.optimization_barrier(jnp.sum(weights, axis=-1, keepdims=True))
    out = jnp.dot(weights.astype(jnp.bfloat16), vh, preferred_element_type=jnp.float32) / total
    return (out, top[:, 0] + jnp.log(total[:, 0]))

def head_backward(args):
    qh, kh, vh, gh, lse, dsum = args
    scores = jnp.dot(qh, kh.T, preferred_element_type=jnp.float32) * HD ** (-0.5)
    probs = jnp.exp(scores - lse[:, None])
    dval = jnp.dot(probs.astype(jnp.bfloat16).T, gh, preferred_element_type=jnp.float32)
    dprobs = jnp.dot(gh, vh.T, preferred_element_type=jnp.float32)
    dscores = (probs * (dprobs - dsum[:, None])).astype(jnp.bfloat16)
    dquery = jnp.dot(dscores, kh, preferred_element_type=jnp.float32) * HD ** (-0.5)
    dkey = jnp.dot(dscores.T, qh, preferred_element_type=jnp.float32) * HD ** (-0.5)
    return (dquery, dkey, dval)

def forward_block(u, mods, w_qkv, w_out):
    normed, nhat, rstd = normalize(u, mods[0], mods[1])
    query = jnp.dot(normed, w_qkv[0], preferred_element_type=jnp.float32).astype(jnp.bfloat16)
    keys = jnp.dot(normed, w_qkv[1], preferred_element_type=jnp.float32).astype(jnp.bfloat16)
    values = jnp.dot(normed, w_qkv[2], preferred_element_type=jnp.float32).astype(jnp.bfloat16)
    out_heads, lse = lax.map(head_forward, (split_heads(query), split_heads(keys), split_heads(values)))
    attn = merge_heads(out_heads).astype(jnp.bfloat16)
    branch = jnp.dot(attn, w_out.T, preferred_element_type=jnp.float32)
    state = (u.astype(jnp.float32) + mods[2] * branch).astype(jnp.bfloat16)
    return (normed, nhat, rstd, query, keys, values, attn, lse, state)

def backward_block(saved, incoming, mods, w_qkv, w_out):
    normed, nhat, rstd, query, keys, values, attn, lse, state = saved
    gated = (mods[2] * incoming.astype(jnp.float32)).astype(jnp.bfloat16)
    attn_grad = jnp.dot(gated, w_out, preferred_element_type=jnp.float32).astype(jnp.bfloat16)
    dsum = lax.optimization_barrier(jnp.sum((attn_grad.astype(jnp.float32) * attn.astype(jnp.float32)).reshape(TOKENS, HEADS, HD), axis=-1)).T
    dq, dk, dv = lax.map(head_backward, (split_heads(query), split_heads(keys), split_heads(values), split_heads(attn_grad), lse, dsum))
    grads = jnp.stack([merge_heads(dq).astype(jnp.bfloat16), merge_heads(dk).astype(jnp.bfloat16), merge_heads(dv).astype(jnp.bfloat16)])
    dnorm = jnp.zeros((TOKENS, D), jnp.float32)
    for index in range(3):
        dnorm = dnorm + jnp.dot(grads[index], w_qkv[index].T, preferred_element_type=jnp.float32)
    scaled = dnorm * (1.0 + mods[1])
    first = lax.optimization_barrier(jnp.mean(scaled, axis=-1, keepdims=True))
    second = lax.optimization_barrier(jnp.mean(scaled * nhat, axis=-1, keepdims=True))
    d_in = incoming.astype(jnp.float32) + rstd * (scaled - first - nhat * second)
    return (d_in, gated, grads)

def reference(latent, hint, timestep, modulation, qkv_weight, out_weight, zero_weight, cotangent):
    pick = (jnp.arange(STEPS, dtype=jnp.int32) == timestep[0]).astype(jnp.float32)
    mods = lax.optimization_barrier(jnp.sum(modulation * pick[None, :, None, None], axis=1))
    first_in = (latent.astype(jnp.float32) + hint.astype(jnp.float32)).astype(jnp.bfloat16)
    control = forward_block(first_in, mods[0], qkv_weight[0], out_weight[0])
    main = forward_block(latent, mods[1], qkv_weight[1], out_weight[1])
    control_out = control[8]
    projected = jnp.dot(control_out, zero_weight.T, preferred_element_type=jnp.float32)
    mixed = (main[8].astype(jnp.float32) + projected).astype(jnp.bfloat16)
    hint_back = jnp.dot(cotangent, zero_weight, preferred_element_type=jnp.float32).astype(jnp.bfloat16)
    d_control, gated, grads = backward_block(control, hint_back, mods[0], qkv_weight[0], out_weight[0])
    d_main, unused_gated, unused_grads = backward_block(main, cotangent, mods[1], qkv_weight[1], out_weight[1])
    latent_grad = (d_control + d_main).reshape(N_ROW, 2, TOK_DEV // 2, D)
    hint_grad = d_control.reshape(N_ROW, 2, TOK_DEV // 2, D)
    qkv_grad = jnp.einsum('tc,pte->cpe', control[0].astype(jnp.float32), grads.astype(jnp.float32), precision=lax.Precision.HIGHEST)
    out_grad = jnp.einsum('tj,ti->ji', gated.astype(jnp.float32), control[6].astype(jnp.float32), precision=lax.Precision.HIGHEST)
    zero_grad = jnp.einsum('tj,ti->ji', cotangent.astype(jnp.float32), control_out.astype(jnp.float32), precision=lax.Precision.HIGHEST)
    return (mixed, latent_grad, hint_grad, qkv_grad, out_grad, zero_grad)
```

```python
import functools
import math

import jax
import jax.numpy as jnp
from jax import lax
from jax.experimental import pallas as pl
from jax.experimental.pallas import tpu as pltpu
from jax.sharding import PartitionSpec as P

HD = 128


EPS = 1e-06

MESH = pl.DeviceIdType.MESH


def place(axes, sizes):
    index = 0
    for axis, size in zip(axes, sizes):
        index = index * size + lax.axis_index(axis)
    return index


def coords(index, axes, sizes):
    spot = {}
    for axis, size in reversed(list(zip(axes, sizes))):
        spot[axis] = lax.rem(index, size)
        index = index // size
    return spot


def exchange_kernel(plans, *refs):
    count = len(plans)
    ins, outs = refs[:count], refs[count : 2 * count]
    sems = refs[2 * count :]
    group = lax.axis_index("group")
    barrier = pltpu.get_barrier_semaphore()
    greeted = 0
    seen = set()
    for kind, axes, sizes, source in plans:
        if axes in seen:
            continue
        seen.add(axes)
        total = math.prod(sizes)
        me = place(axes, sizes)
        for step in range(1, total):
            pl.semaphore_signal(
                barrier,
                inc=1,
                device_id=coords(lax.rem(me + step, total), axes, sizes),
                device_id_type=MESH,
            )
        greeted += total - 1
    pl.semaphore_wait(barrier, greeted)

    def each(plan, number, action):
        kind, axes, sizes, source = plan
        x, out = ins[number], outs[number]
        send, recv, local = sems[3 * number : 3 * number + 3]
        total = math.prod(sizes)
        me = place(axes, sizes)
        spread = kind.startswith("spread")
        dealt = kind.endswith("deal")
        per = total // sizes[0] if spread else total
        mine = lax.rem(me, per)

        def when(index):
            if source is None:
                return None
            if spread:
                return index // per == source
            return group == source

        def guarded(condition, work):
            if condition is None:
                work()
            else:
                pl.when(condition)(work)

        def own():
            copy = pltpu.make_async_copy(x.at[me] if dealt else x, out.at[mine], local)
            copy.start() if action == "start" else copy.wait()

        for step in range(1, total):
            there = lax.rem(me + step, total)
            origin = lax.rem(me + total - step, total)

            def copy_of(slot, block):
                return pltpu.make_async_remote_copy(
                    src_ref=x.at[block] if dealt else x,
                    dst_ref=out.at[slot],
                    send_sem=send.at[step],
                    recv_sem=recv.at[step],
                    device_id=coords(there, axes, sizes),
                    device_id_type=MESH,
                )

            if action == "start":
                guarded(when(me), lambda: copy_of(mine, there).start())
            else:
                guarded(when(me), lambda: copy_of(mine, there).wait_send())
                guarded(
                    when(origin), lambda: copy_of(lax.rem(origin, per), there).wait_recv()
                )
        guarded(when(me), own)

    for number, plan in enumerate(plans):
        each(plan, number, "start")
    for number, plan in enumerate(plans):
        each(plan, number, "wait")


def exchange(number, name, *wants):
    plans, arrays, shapes, scratch = [], [], [], []
    for kind, x, axes, source in wants:
        sizes = tuple(lax.axis_size(axis) for axis in axes)
        total = math.prod(sizes)
        per = total // sizes[0] if kind.startswith("spread") else total
        block = x.shape[1:] if kind.endswith("deal") else x.shape
        plans.append((kind, axes, sizes, source))
        arrays.append(x)
        shapes.append(jax.ShapeDtypeStruct((per,) + block, x.dtype))
        scratch += [
            pltpu.SemaphoreType.DMA((total,)),
            pltpu.SemaphoreType.DMA((total,)),
            pltpu.SemaphoreType.DMA,
        ]
    return pl.pallas_call(
        functools.partial(exchange_kernel, tuple(plans)),
        out_shape=shapes,
        in_specs=[pl.BlockSpec(memory_space=pl.ANY)] * len(arrays),
        out_specs=[pl.BlockSpec(memory_space=pl.ANY)] * len(arrays),
        scratch_shapes=scratch,
        compiler_params=pltpu.CompilerParams(collective_id=number, has_side_effects=True),
        name=name,
    )(*arrays)


def attention_kernel(q_ref, k_ref, v_ref, g_ref, o_ref, dq_ref, dk_ref, dv_ref):
    scaling = HD ** (-0.5)
    query, cot = q_ref[...], g_ref[...]
    keys = k_ref[...].reshape(-1, HD)
    values = v_ref[...].reshape(-1, HD)
    last = (((1,), (1,)), ((), ()))
    first = (((0,), (0,)), ((), ()))
    scores = lax.dot_general(query, keys, last, preferred_element_type=jnp.float32) * scaling
    top = jnp.max(scores, axis=-1, keepdims=True)
    weights = jnp.exp(scores - top)
    inverse = 1.0 / jnp.sum(weights, axis=-1, keepdims=True)
    out = jnp.dot(weights.astype(jnp.bfloat16), values, preferred_element_type=jnp.float32)
    out = (out * inverse).astype(jnp.bfloat16)
    o_ref[...] = out
    dsum = jnp.sum(cot.astype(jnp.float32) * out.astype(jnp.float32), axis=-1, keepdims=True)
    probs = weights * inverse
    dprobs = lax.dot_general(cot, values, last, preferred_element_type=jnp.float32)
    dscores = (probs * (dprobs - dsum)).astype(jnp.bfloat16)
    dquery = jnp.dot(dscores, keys, preferred_element_type=jnp.float32) * scaling
    dq_ref[...] = dquery.astype(jnp.bfloat16)
    dkey = lax.dot_general(dscores, query, first, preferred_element_type=jnp.float32) * scaling
    dk_ref[...] = dkey.astype(jnp.bfloat16).reshape(dk_ref.shape)
    dval = lax.dot_general(
        probs.astype(jnp.bfloat16), cot, first, preferred_element_type=jnp.float32
    )
    dv_ref[...] = dval.astype(jnp.bfloat16).reshape(dv_ref.shape)


def attention(query, keys, values, cot):
    tok, width = query.shape
    rows = keys.shape[0]
    own = pl.BlockSpec((tok, HD), lambda h: (0, h))
    every = pl.BlockSpec((rows, tok, HD), lambda h: (0, 0, h))
    small = jax.ShapeDtypeStruct((tok, width), jnp.bfloat16)
    large = jax.ShapeDtypeStruct((rows, tok, width), jnp.bfloat16)
    return pl.pallas_call(
        attention_kernel,
        grid=(width // HD,),
        out_shape=[small, small, large, large],
        in_specs=[own, every, every, own],
        out_specs=[own, own, every, every],
        compiler_params=pltpu.CompilerParams(vmem_limit_bytes=50 * 1024 * 1024),
        name="attention",
    )(query, keys, values, cot)


def from_partner(block, axis, distance):
    count = lax.axis_size(axis)
    route = []
    for low in range(count):
        high = low | 1 << distance
        if high != low and high < count:
            route += [(low, high), (high, low)]
    return lax.ppermute(block, axis, route)


def dot(a, b, dims):
    return lax.dot_general(a, b, (dims, ((), ())), preferred_element_type=jnp.float32)


def on_device(latent, hint, timestep, modulation, qkv_weight, out_weight, zero_weight, cotangent):
    f32, bf16 = jnp.float32, jnp.bfloat16
    tok, width = latent.shape
    half = tok // 2
    n_head, n_row = lax.axis_size("head"), lax.axis_size("row")
    full_width = n_head * width
    parts = 2 * n_row
    plane = ("group", "row")
    group_pos = lax.axis_index("group")
    control = group_pos == 0
    head_pos = lax.axis_index("head")
    steps_count = modulation.shape[1]
    pick = (lax.broadcasted_iota(jnp.int32, (steps_count,), 0) == timestep[0]).astype(f32)
    mods = jnp.sum(modulation[0] * pick[:, None, None], axis=0)
    shift, scale, gate = (mods[0], mods[1], mods[2])
    gate_dev = lax.dynamic_slice_in_dim(gate, head_pos * width, width, 0)
    scale_dev = lax.dynamic_slice_in_dim(scale, head_pos * width, width, 0)
    w_qkv, w_out = qkv_weight[0], out_weight[0]

    def widen(blocks):
        return blocks.transpose(1, 0, 2).reshape(blocks.shape[1], -1)

    def deal_out(x):
        return x.reshape(x.shape[0], parts, -1).transpose(1, 0, 2)

    summed = (latent.astype(f32) + hint.astype(f32)).astype(bf16)
    inputs = jnp.where(control, summed, latent)
    cot_own = lax.dynamic_slice_in_dim(cotangent, group_pos * half, half, 0)
    whole, cot_half = exchange(
        0,
        "gather_inputs",
        ("gather", cot_own, ("head",), None),
        ("gather", inputs, ("head",), None),
    )[::-1]
    cot_half = widen(cot_half)
    hint_half = dot(cot_half, zero_weight, ((1,), (0,))).astype(bf16)
    hint_other = from_partner(hint_half, "group", 0)
    cot_other = from_partner(cot_half, "group", 0)

    whole_f = widen(whole).astype(f32)
    mean = jnp.mean(whole_f, axis=-1, keepdims=True)
    centred = whole_f - mean
    var = jnp.mean(centred * centred, axis=-1, keepdims=True)
    rstd = lax.rsqrt(var + EPS)
    nhat = centred * rstd
    normed = (nhat * (1.0 + scale) + shift).astype(bf16)
    query, keys, values = [
        dot(normed, w_qkv[index], ((1,), (0,))).astype(bf16) for index in range(3)
    ]

    hint_back = jnp.concatenate([hint_half, hint_other])
    incoming = jnp.where(control, hint_back, cotangent)
    gated = (gate_dev * hint_back.astype(f32)).astype(bf16)
    gated_blocks, all_keys, all_values, cot_parts, normed_parts = exchange(
        1,
        "gather_keys",
        ("gather", gated, ("head",), 0),
        ("gather", keys, ("row",), None),
        ("gather", values, ("row",), None),
        ("deal", deal_out(cot_half), plane, None),
        ("spread_deal", deal_out(normed), plane, 0),
    )
    gated_main = (gate * jnp.concatenate([cot_other, cot_half]).astype(f32)).astype(bf16)
    gated_full = jnp.where(control, widen(gated_blocks), gated_main)
    attn_grad = dot(gated_full, w_out, ((1,), (0,))).astype(bf16)
    attn, dquery, key_terms, value_terms = attention(query, all_keys, all_values, attn_grad)
    branch_term = jnp.stack(
        [
            dot(attn, w_out[index * width : (index + 1) * width], ((1,), (1,))).astype(bf16)
            for index in range(n_head)
        ]
    )
    branch_parts, key_parts, value_parts, all_attn, gated_parts = exchange(
        2,
        "sum_branch",
        ("deal", branch_term, ("head",), None),
        ("deal", key_terms, ("row",), None),
        ("deal", value_terms, ("row",), None),
        ("spread", attn, plane, 0),
        ("spread_deal", deal_out(gated_full), plane, 0),
    )
    branch = jnp.sum(branch_parts.astype(f32), axis=0)
    state = (inputs.astype(f32) + gate_dev * branch).astype(bf16)
    dkey = jnp.sum(key_parts.astype(f32), axis=0).astype(bf16)
    dval = jnp.sum(value_parts.astype(f32), axis=0).astype(bf16)
    grads = jnp.stack([dquery, dkey, dval])

    scaled_nhat = nhat * (1.0 + scale)
    terms = []
    first, second = 0.0, 0.0
    for index in range(n_head):
        cols = slice(index * width, (index + 1) * width)
        term = sum(dot(grads[c], w_qkv[c, cols], ((1,), (1,))) for c in range(3))
        first = first + jnp.sum(term * (1.0 + scale[cols]), axis=-1)
        second = second + jnp.sum(term * scaled_nhat[:, cols], axis=-1)
        terms.append(term.astype(bf16))
    norm_parts, sum_parts, all_state, near_grads, main_state = exchange(
        3,
        "sum_norm",
        ("deal", jnp.stack(terms), ("head",), None),
        ("gather", jnp.stack([first, second]), ("head",), None),
        ("spread", state, plane, 0),
        ("spread", grads, ("group",), 0),
        ("spread", state[:half], ("group",), 1),
    )
    dnorm = jnp.sum(norm_parts.astype(f32), axis=0)
    sums = jnp.sum(sum_parts, axis=0) / full_width
    nhat_dev = lax.dynamic_slice_in_dim(nhat, head_pos * width, width, 1)
    scaled = dnorm * (1.0 + scale_dev)
    d_in = incoming.astype(f32) + rstd * (
        scaled - sums[0][:, None] - nhat_dev * sums[1][:, None]
    )
    own_half = lax.dynamic_slice_in_dim(d_in, group_pos * half, half, 0)
    sent_half = lax.dynamic_slice_in_dim(d_in, (1 - group_pos) * half, half, 0)

    row_pos = lax.axis_index("row")
    state_row = lax.dynamic_index_in_dim(all_state, row_pos, 0, keepdims=False)
    state_half = lax.dynamic_slice_in_dim(state_row, group_pos * half, half, 0)
    hint_term = jnp.stack(
        [
            dot(state_half, zero_weight[index * width : (index + 1) * width], ((1,), (1,)))
            .astype(bf16)
            for index in range(n_head)
        ]
    )
    hint_parts, other_parts, all_grads = exchange(
        4,
        "sum_hint",
        ("deal", hint_term, ("head",), None),
        ("gather", sent_half.astype(bf16), ("group",), None),
        ("gather", near_grads[0], ("row",), None),
    )
    projected = jnp.sum(hint_parts.astype(f32), axis=0)
    main_half = jnp.where(control, main_state[0], state[half:])
    mixed_half = (main_half.astype(f32) + projected).astype(bf16)
    mixed_other = from_partner(mixed_half, "group", 0)
    mixed = jnp.where(
        control,
        jnp.concatenate([mixed_half, mixed_other]),
        jnp.concatenate([mixed_other, mixed_half]),
    )
    other_half = lax.dynamic_index_in_dim(other_parts, 1 - group_pos, 0, keepdims=False).astype(f32)
    latent_grad = (own_half + other_half)[None, None]
    hint_grad = jnp.where(control, own_half, other_half)[None, None]

    normed_cols = normed_parts.reshape(n_row * tok, -1)
    qkv_grad = jnp.stack(
        [
            dot(normed_cols, all_grads[:, c].reshape(n_row * tok, width), ((0,), (0,)))
            for c in range(3)
        ],
        axis=1,
    )
    out_grad = dot(
        gated_parts.reshape(n_row * tok, -1), all_attn.reshape(n_row * tok, width), ((0,), (0,))
    )
    cot_cols = cot_parts.reshape(2, n_row, half, -1).transpose(1, 0, 2, 3)
    zero_grad = dot(
        cot_cols.reshape(n_row * tok, -1), all_state.reshape(n_row * tok, width), ((0,), (0,))
    )
    return (mixed, latent_grad, hint_grad, qkv_grad, out_grad, zero_grad)


def solution(mesh):
    placed = (
        P("row", "head"),
        P("row", "head"),
        P(),
        P("group", None, None, None),
        P("group", None, None, "head"),
        P("group", None, "head"),
        P(None, "head"),
        P("row", "head"),
    )
    return jax.shard_map(
        on_device,
        mesh=mesh,
        in_specs=placed,
        out_specs=(
            P("row", "head"),
            P("row", "group", None, "head"),
            P("row", "group", None, "head"),
            P(("group", "row"), None, "head"),
            P(("group", "row"), "head"),
            P(("group", "row"), "head"),
        ),
        check_vma=False,
    )
```

```python
import functools

import jax
import jax.numpy as jnp
from jax import lax
from jax.experimental import pallas as pl
from jax.experimental.pallas import tpu as pltpu
from jax.sharding import PartitionSpec as P

HD = 128


EPS = 1e-06

MESH = pl.DeviceIdType.MESH


def greet(peers):
    barrier = pltpu.get_barrier_semaphore()
    for peer in peers:
        pl.semaphore_signal(barrier, inc=1, device_id={"head": peer}, device_id_type=MESH)
    pl.semaphore_wait(barrier, len(peers))


def others(me, n):
    return [lax.rem(me + step, n) for step in range(1, n)]


def line_gather_kernel(n, sources, *refs):
    count = len(sources)
    ins, outs, sems = refs[:count], refs[count : 2 * count], refs[2 * count :]
    me = lax.axis_index("head")
    greet(others(me, n))
    group = lax.axis_index("group")

    def copy_of(number, block, way):
        x, out = ins[number], outs[number]
        send, recv = sems[3 * number : 3 * number + 2]
        side = 0 if way > 0 else 1
        return pltpu.make_async_remote_copy(
            src_ref=out.at[block],
            dst_ref=out.at[block],
            send_sem=send.at[side, block],
            recv_sem=recv.at[side, block],
            device_id={"head": me + way},
            device_id_type=MESH,
        )

    def own_copy(number, way):
        x, out = ins[number], outs[number]
        send, recv = sems[3 * number : 3 * number + 2]
        side = 0 if way > 0 else 1
        return pltpu.make_async_remote_copy(
            src_ref=x,
            dst_ref=out.at[me],
            send_sem=send.at[side, me],
            recv_sem=recv.at[side, me],
            device_id={"head": me + way},
            device_id_type=MESH,
        )

    def active(number, work):
        source = sources[number]
        if source is None:
            work()
        else:
            pl.when(group == source)(work)

    def local_copy(number):
        return pltpu.make_async_copy(ins[number], outs[number].at[me], sems[3 * number + 2])

    def begin(number):
        pl.when(me < n - 1)(lambda: own_copy(number, 1).start())
        pl.when(me > 0)(lambda: own_copy(number, -1).start())
        local_copy(number).start()

    def hop(number, distance):
        @pl.when(me >= distance)
        def _():
            copy = copy_of(number, me - distance, 1)
            copy.wait_recv()
            pl.when(me < n - 1)(copy.start)

        @pl.when(me + distance < n)
        def _():
            copy = copy_of(number, me + distance, -1)
            copy.wait_recv()
            pl.when(me > 0)(copy.start)

    def finish(number):
        for distance in range(n):
            @pl.when((me >= distance) & (me < n - 1))
            def _():
                copy_of(number, me - distance, 1).wait_send()

            @pl.when((me + distance < n) & (me > 0))
            def _():
                copy_of(number, me + distance, -1).wait_send()
        local_copy(number).wait()

    for number in range(count):
        active(number, functools.partial(begin, number))
    for distance in range(1, n):
        for number in range(count):
            active(number, functools.partial(hop, number, distance))
    for number in range(count):
        active(number, functools.partial(finish, number))


def line_gather(number, name, *wants):
    n = lax.axis_size("head")
    scratch = []
    for x, source in wants:
        scratch += [
            pltpu.SemaphoreType.DMA((2, n)),
            pltpu.SemaphoreType.DMA((2, n)),
            pltpu.SemaphoreType.DMA,
        ]
    arrays = [x for x, source in wants]
    sent = sum(x.size * x.dtype.itemsize for x in arrays)
    return pl.pallas_call(
        functools.partial(line_gather_kernel, n, tuple(source for x, source in wants)),
        out_shape=[jax.ShapeDtypeStruct((n,) + x.shape, x.dtype) for x in arrays],
        in_specs=[pl.BlockSpec(memory_space=pl.ANY)] * len(arrays),
        out_specs=[pl.BlockSpec(memory_space=pl.ANY)] * len(arrays),
        scratch_shapes=scratch,
        compiler_params=pltpu.CompilerParams(collective_id=number, has_side_effects=True),
        cost_estimate=pl.CostEstimate(flops=0, bytes_accessed=200 * sent, transcendentals=0),
        name=name,
    )(*arrays)


def line_sum_kernel(n, small, *refs):
    if small:
        x, extra, total, extras, *scratch = refs
        extra_send, extra_recv, extra_local = scratch[-3:]
    else:
        x, total, *scratch = refs
    sends, recvs, send, recv = scratch[:4]
    me = lax.axis_index("head")
    greet(others(me, n))
    f32 = jnp.float32

    def extra_copy(step):
        return pltpu.make_async_remote_copy(
            src_ref=extra,
            dst_ref=extras.at[me],
            send_sem=extra_send.at[step],
            recv_sem=extra_recv.at[step],
            device_id={"head": lax.rem(me + step, n)},
            device_id_type=MESH,
        )

    if small:
        for step in range(1, n):
            extra_copy(step).start()
        extra_own = pltpu.make_async_copy(extra, extras.at[me], extra_local)
        extra_own.start()

    def copy_of(side, block):
        return pltpu.make_async_remote_copy(
            src_ref=sends.at[side, block],
            dst_ref=recvs.at[side, block],
            send_sem=send.at[side, block],
            recv_sem=recv.at[side, block],
            device_id={"head": me + (1 if side == 0 else -1)},
            device_id_type=MESH,
        )

    def pass_on(side, block, inner):
        copy = copy_of(side, block)

        @pl.when(inner)
        def _():
            copy.wait_recv()
            sends[side, block] = (
                x[block].astype(f32) + recvs[side, block].astype(f32)
            ).astype(sends.dtype)

        @pl.when(jnp.logical_not(inner))
        def _():
            sends[side, block] = x[block]

        copy.start()

    for step in range(n - 1):
        high, low = n - 1 - step, step
        pl.when(me < high)(lambda: pass_on(0, high, me > 0))
        pl.when(me > low)(lambda: pass_on(1, low, me < n - 1))

    total[...] = x[me].astype(f32)

    @pl.when(me > 0)
    def _():
        copy_of(0, me).wait_recv()
        total[...] += recvs[0, me].astype(f32)

    @pl.when(me < n - 1)
    def _():
        copy_of(1, me).wait_recv()
        total[...] += recvs[1, me].astype(f32)

    for step in range(n - 1):
        high, low = n - 1 - step, step
        pl.when(me < high)(lambda: copy_of(0, high).wait_send())
        pl.when(me > low)(lambda: copy_of(1, low).wait_send())
    if small:
        for step in range(1, n):
            origin = lax.rem(me + n - step, n)
            extra_copy(step).wait_send()
            pltpu.make_async_remote_copy(
                src_ref=extra,
                dst_ref=extras.at[origin],
                send_sem=extra_send.at[step],
                recv_sem=extra_recv.at[step],
                device_id={"head": origin},
                device_id_type=MESH,
            ).wait_recv()
        extra_own.wait()


def line_sum(number, name, x, extra=None):
    n, block = x.shape[0], x.shape[1:]
    small = extra is not None
    arrays = [x, extra] if small else [x]
    shapes = [jax.ShapeDtypeStruct(block, jnp.float32)]
    scratch = [
        pltpu.VMEM((2,) + x.shape, x.dtype),
        pltpu.VMEM((2,) + x.shape, x.dtype),
        pltpu.SemaphoreType.DMA((2, n)),
        pltpu.SemaphoreType.DMA((2, n)),
    ]
    if small:
        shapes.append(jax.ShapeDtypeStruct((n,) + extra.shape, extra.dtype))
        scratch += [
            pltpu.SemaphoreType.DMA((n,)),
            pltpu.SemaphoreType.DMA((n,)),
            pltpu.SemaphoreType.DMA,
        ]
    return pl.pallas_call(
        functools.partial(line_sum_kernel, n, small),
        out_shape=shapes,
        in_specs=[pl.BlockSpec(memory_space=pltpu.VMEM)] * len(arrays),
        out_specs=[pl.BlockSpec(memory_space=pltpu.VMEM)] * len(shapes),
        scratch_shapes=scratch,
        compiler_params=pltpu.CompilerParams(
            collective_id=number, has_side_effects=True, vmem_limit_bytes=40 * 1024 * 1024
        ),
        cost_estimate=pl.CostEstimate(
            flops=0, bytes_accessed=50 * x.size * x.dtype.itemsize, transcendentals=0
        ),
        name=name,
    )(*arrays)


def attention_kernel(q_ref, k_ref, v_ref, g_ref, o_ref, dq_ref, dk_ref, dv_ref):
    scaling = HD ** (-0.5)
    query, cot = q_ref[...], g_ref[...]
    keys = k_ref[...].reshape(-1, HD)
    values = v_ref[...].reshape(-1, HD)
    last = (((1,), (1,)), ((), ()))
    first = (((0,), (0,)), ((), ()))
    scores = lax.dot_general(query, keys, last, preferred_element_type=jnp.float32) * scaling
    top = jnp.max(scores, axis=-1, keepdims=True)
    weights = jnp.exp(scores - top)
    inverse = 1.0 / jnp.sum(weights, axis=-1, keepdims=True)
    out = jnp.dot(weights.astype(jnp.bfloat16), values, preferred_element_type=jnp.float32)
    out = (out * inverse).astype(jnp.bfloat16)
    o_ref[...] = out
    dsum = jnp.sum(cot.astype(jnp.float32) * out.astype(jnp.float32), axis=-1, keepdims=True)
    probs = weights * inverse
    dprobs = lax.dot_general(cot, values, last, preferred_element_type=jnp.float32)
    dscores = (probs * (dprobs - dsum)).astype(jnp.bfloat16)
    dquery = jnp.dot(dscores, keys, preferred_element_type=jnp.float32) * scaling
    dq_ref[...] = dquery.astype(jnp.bfloat16)
    dkey = lax.dot_general(dscores, query, first, preferred_element_type=jnp.float32) * scaling
    dk_ref[...] = dkey.astype(jnp.bfloat16).reshape(dk_ref.shape)
    dval = lax.dot_general(
        probs.astype(jnp.bfloat16), cot, first, preferred_element_type=jnp.float32
    )
    dv_ref[...] = dval.astype(jnp.bfloat16).reshape(dv_ref.shape)


def attention(query, keys, values, cot):
    tok, width = query.shape
    rows = keys.shape[0]
    own = pl.BlockSpec((tok, HD), lambda h: (0, h))
    every = pl.BlockSpec((rows, tok, HD), lambda h: (0, 0, h))
    small = jax.ShapeDtypeStruct((tok, width), jnp.bfloat16)
    large = jax.ShapeDtypeStruct((rows, tok, width), jnp.bfloat16)
    return pl.pallas_call(
        attention_kernel,
        grid=(width // HD,),
        out_shape=[small, small, large, large],
        in_specs=[own, every, every, own],
        out_specs=[own, own, every, every],
        compiler_params=pltpu.CompilerParams(vmem_limit_bytes=50 * 1024 * 1024),
        name="attention",
    )(query, keys, values, cot)


def dot(a, b, dims):
    return lax.dot_general(a, b, (dims, ((), ())), preferred_element_type=jnp.float32)


def row_bits():
    bits, bit = [], lax.axis_size("row") // 2
    while bit:
        bits.append(bit)
        bit //= 2
    return bits


def row_swap(x, bit):
    return lax.ppermute(x, "row", [(row, row ^ bit) for row in range(lax.axis_size("row"))])


def cube_gather(x, dim):
    for bit in row_bits():
        x = jnp.concatenate([x, row_swap(x, bit)], axis=dim)
    return x


def cube_deal(x):
    row = lax.axis_index("row")
    for bit in row_bits():
        cols = x.shape[1] // 2
        upper = (row // bit) % 2 == 1
        low, high = x[:, :cols], x[:, cols:]
        kept, sent = jnp.where(upper, high, low), jnp.where(upper, low, high)
        x = jnp.concatenate([kept, row_swap(sent, bit)], axis=0)
    return x


def on_device(latent, hint, timestep, modulation, qkv_weight, out_weight, zero_weight, cotangent):
    f32, bf16 = jnp.float32, jnp.bfloat16
    tok, width = latent.shape
    half = tok // 2
    n_head, n_row = lax.axis_size("head"), lax.axis_size("row")
    full_width = n_head * width
    group_pos = lax.axis_index("group")
    control = group_pos == 0
    head_pos = lax.axis_index("head")
    steps_count = modulation.shape[1]
    pick = (lax.broadcasted_iota(jnp.int32, (steps_count,), 0) == timestep[0]).astype(f32)
    mods = jnp.sum(modulation[0] * pick[:, None, None], axis=0)
    shift, scale, gate = (mods[0], mods[1], mods[2])
    gate_dev = lax.dynamic_slice_in_dim(gate, head_pos * width, width, 0)
    scale_dev = lax.dynamic_slice_in_dim(scale, head_pos * width, width, 0)
    w_qkv, w_out = qkv_weight[0], out_weight[0]

    def widen(blocks):
        return jnp.concatenate([blocks[index] for index in range(n_head)], axis=1)

    def swap(x):
        return lax.ppermute(x, "group", [(0, 1), (1, 0)])

    def near(x):
        return jnp.where(control, x, lax.ppermute(x, "group", [(0, 1)]))

    def near_cols(x):
        cols = x.shape[1] // 2
        return jnp.where(control, x[:, :cols], lax.ppermute(x[:, cols:], "group", [(0, 1)]))

    def head_terms(x, weight):
        return jnp.stack(
            [
                dot(x, weight[index * width : (index + 1) * width], ((1,), (1,))).astype(bf16)
                for index in range(n_head)
            ]
        )

    summed = (latent.astype(f32) + hint.astype(f32)).astype(bf16)
    inputs = jnp.where(control, summed, latent)
    cot_own = jnp.where(control, cotangent[:half], cotangent[half:])
    cot_half, whole = line_gather(0, "gather_inputs", (cot_own, None), (inputs, None))
    cot_half = widen(cot_half)
    hint_half = dot(cot_half, zero_weight, ((1,), (0,))).astype(bf16)
    hint_other = swap(hint_half)
    cot_other = swap(cot_half)

    whole_f = widen(whole).astype(f32)
    mean = jnp.mean(whole_f, axis=-1, keepdims=True)
    centred = whole_f - mean
    var = jnp.mean(centred * centred, axis=-1, keepdims=True)
    rstd = lax.rsqrt(var + EPS)
    nhat = centred * rstd
    normed = (nhat * (1.0 + scale) + shift).astype(bf16)
    keys, values, query = [
        dot(normed, w_qkv[index], ((1,), (0,))).astype(bf16) for index in (1, 2, 0)
    ]
    all_keys = cube_gather(keys[None], 0)
    all_values = cube_gather(values[None], 0)

    hint_back = jnp.concatenate([hint_half, hint_other])
    incoming = jnp.where(control, hint_back, cotangent)
    gated = (gate_dev * hint_back.astype(f32)).astype(bf16)
    (gated_blocks,) = line_gather(1, "gather_gated", (gated, 0))
    cot_full = jnp.where(
        control,
        jnp.concatenate([cot_half, cot_other]),
        jnp.concatenate([cot_other, cot_half]),
    )
    gated_main = (gate * cot_full.astype(f32)).astype(bf16)
    gated_full = jnp.where(control, widen(gated_blocks), gated_main)
    attn_grad = dot(gated_full, w_out, ((1,), (0,))).astype(bf16)
    attn, dquery, key_terms, value_terms = attention(query, all_keys, all_values, attn_grad)

    bits = row_bits()

    def row_sum(x):
        blocks = [x[index] for index in range(n_row)]
        for bit in bits[::-1]:
            count = len(blocks) // 2
            other = row_swap(jnp.stack(blocks[count:]), bit)
            blocks = [
                (blocks[index].astype(f32) + other[index].astype(f32)).astype(bf16)
                for index in range(count)
            ]
        return blocks[0]

    dkey, dval = row_sum(key_terms), row_sum(value_terms)
    (branch,) = line_sum(2, "sum_branch", head_terms(attn, w_out))
    state = (inputs.astype(f32) + gate_dev * branch).astype(bf16)
    grads = [dquery, dkey, dval]

    scaled_nhat = nhat * (1.0 + scale)
    terms = []
    first, second = 0.0, 0.0
    for index in range(n_head):
        cols = slice(index * width, (index + 1) * width)
        term = sum(dot(grads[c], w_qkv[c, cols], ((1,), (1,))) for c in range(3))
        first = first + jnp.sum(term * (1.0 + scale[cols]), axis=-1)
        second = second + jnp.sum(term * scaled_nhat[:, cols], axis=-1)
        terms.append(term.astype(bf16))
    sums = jnp.concatenate([first[None], second[None], jnp.zeros((6, tok), f32)])
    dnorm, sum_parts = line_sum(3, "sum_norm", jnp.stack(terms), sums)
    sums = jnp.sum(sum_parts, axis=0) / full_width
    nhat_dev = lax.dynamic_slice_in_dim(nhat, head_pos * width, width, 1)
    scaled = dnorm * (1.0 + scale_dev)
    d_in = incoming.astype(f32) + rstd * (
        scaled - sums[0][:, None] - nhat_dev * sums[1][:, None]
    )
    own_half = jnp.where(control, d_in[:half], d_in[half:])
    sent_half = jnp.where(control, d_in[half:], d_in[:half])
    other_half = swap(sent_half.astype(bf16)).astype(f32)
    latent_grad = (own_half + other_half)[None, None]
    hint_grad = jnp.where(control, own_half, other_half)[None, None]

    near_state = near(state)
    state_half = jnp.where(control, near_state[:half], near_state[half:])
    (projected,) = line_sum(4, "sum_hint", head_terms(state_half, zero_weight))
    main_state = lax.ppermute(state[:half], "group", [(1, 0)])
    main_half = jnp.where(control, main_state, state[half:])
    mixed_half = (main_half.astype(f32) + projected).astype(bf16)
    mixed_other = swap(mixed_half)
    mixed = jnp.where(
        control,
        jnp.concatenate([mixed_half, mixed_other]),
        jnp.concatenate([mixed_other, mixed_half]),
    )

    tokens = ((0,), (0,))
    normed_cols = cube_deal(near_cols(normed))
    qkv_grad = jnp.stack(
        [dot(normed_cols, cube_gather(near(grads[c]), 0), tokens) for c in range(3)], axis=1
    )
    out_grad = dot(cube_deal(near_cols(gated_full)), cube_gather(near(attn), 0), tokens)
    cot_cols = jnp.where(
        control, cot_full[:, : full_width // 2], cot_full[:, full_width // 2 :]
    )
    zero_grad = dot(cube_deal(cot_cols), cube_gather(near_state, 0), tokens)
    return (mixed, latent_grad, hint_grad, qkv_grad, out_grad, zero_grad)


def solution(mesh):
    placed = (
        P("row", "head"),
        P("row", "head"),
        P(),
        P("group", None, None, None),
        P("group", None, None, "head"),
        P("group", None, "head"),
        P(None, "head"),
        P("row", "head"),
    )
    return jax.shard_map(
        on_device,
        mesh=mesh,
        in_specs=placed,
        out_specs=(
            P("row", "head"),
            P("row", "group", None, "head"),
            P("row", "group", None, "head"),
            P(("group", "row"), None, "head"),
            P(("group", "row"), "head"),
            P(("group", "row"), "head"),
        ),
        check_vma=False,
    )
```

```python
import functools

import jax
import jax.numpy as jnp
from jax import lax
from jax.experimental import pallas as pl
from jax.experimental.pallas import tpu as pltpu
from jax.sharding import PartitionSpec as P

HD = 128


EPS = 1e-06

MESH = pl.DeviceIdType.MESH


def greet(peers, row_peers=()):
    barrier = pltpu.get_barrier_semaphore()
    for peer in peers:
        pl.semaphore_signal(barrier, inc=1, device_id={"head": peer}, device_id_type=MESH)
    for peer in row_peers:
        pl.semaphore_signal(barrier, inc=1, device_id={"row": peer}, device_id_type=MESH)
    pl.semaphore_wait(barrier, len(peers) + len(row_peers))


def row_partner(bit):
    row = lax.axis_index("row")
    return row + bit - 2 * bit * ((row // bit) % 2)


def others(me, n):
    return [lax.rem(me + step, n) for step in range(1, n)]


def line_gather_kernel(n, sources, *refs):
    count = len(sources)
    ins, outs, sems = refs[:count], refs[count : 2 * count], refs[2 * count :]
    me = lax.axis_index("head")
    greet(others(me, n))
    group = lax.axis_index("group")

    def copy_of(number, block, way):
        x, out = ins[number], outs[number]
        send, recv = sems[3 * number : 3 * number + 2]
        side = 0 if way > 0 else 1
        return pltpu.make_async_remote_copy(
            src_ref=out.at[block],
            dst_ref=out.at[block],
            send_sem=send.at[side, block],
            recv_sem=recv.at[side, block],
            device_id={"head": me + way},
            device_id_type=MESH,
        )

    def own_copy(number, way):
        x, out = ins[number], outs[number]
        send, recv = sems[3 * number : 3 * number + 2]
        side = 0 if way > 0 else 1
        return pltpu.make_async_remote_copy(
            src_ref=x,
            dst_ref=out.at[me],
            send_sem=send.at[side, me],
            recv_sem=recv.at[side, me],
            device_id={"head": me + way},
            device_id_type=MESH,
        )

    def active(number, work):
        source = sources[number]
        if source is None:
            work()
        else:
            pl.when(group == source)(work)

    def local_copy(number):
        return pltpu.make_async_copy(ins[number], outs[number].at[me], sems[3 * number + 2])

    def begin(number):
        pl.when(me < n - 1)(lambda: own_copy(number, 1).start())
        pl.when(me > 0)(lambda: own_copy(number, -1).start())
        local_copy(number).start()

    def hop(number, distance):
        @pl.when(me >= distance)
        def _():
            copy = copy_of(number, me - distance, 1)
            copy.wait_recv()
            pl.when(me < n - 1)(copy.start)

        @pl.when(me + distance < n)
        def _():
            copy = copy_of(number, me + distance, -1)
            copy.wait_recv()
            pl.when(me > 0)(copy.start)

    def finish(number):
        for distance in range(n):
            @pl.when((me >= distance) & (me < n - 1))
            def _():
                copy_of(number, me - distance, 1).wait_send()

            @pl.when((me + distance < n) & (me > 0))
            def _():
                copy_of(number, me + distance, -1).wait_send()
        local_copy(number).wait()

    for number in range(count):
        active(number, functools.partial(begin, number))
    for distance in range(1, n):
        for number in range(count):
            active(number, functools.partial(hop, number, distance))
    for number in range(count):
        active(number, functools.partial(finish, number))


def line_gather(number, name, *wants):
    n = lax.axis_size("head")
    scratch = []
    for x, source in wants:
        scratch += [
            pltpu.SemaphoreType.DMA((2, n)),
            pltpu.SemaphoreType.DMA((2, n)),
            pltpu.SemaphoreType.DMA,
        ]
    arrays = [x for x, source in wants]
    sent = sum(x.size * x.dtype.itemsize for x in arrays)
    return pl.pallas_call(
        functools.partial(line_gather_kernel, n, tuple(source for x, source in wants)),
        out_shape=[jax.ShapeDtypeStruct((n,) + x.shape, x.dtype) for x in arrays],
        in_specs=[pl.BlockSpec(memory_space=pl.ANY)] * len(arrays),
        out_specs=[pl.BlockSpec(memory_space=pl.ANY)] * len(arrays),
        scratch_shapes=scratch,
        compiler_params=pltpu.CompilerParams(collective_id=number, has_side_effects=True),
        cost_estimate=pl.CostEstimate(flops=0, bytes_accessed=200 * sent, transcendentals=0),
        name=name,
    )(*arrays)


def line_sum_kernel(n, small, bits, *refs):
    if bits:
        x, keyed, total, key_total, *scratch = refs
        acc, taken, key_send, key_recv = scratch[-4:]
    elif small:
        x, extra, total, extras, *scratch = refs
        extra_send, extra_recv, extra_local = scratch[-3:]
    else:
        x, total, *scratch = refs
    sends, recvs, send, recv = scratch[:4]
    me = lax.axis_index("head")
    greet(others(me, n), [row_partner(bit) for bit in bits])
    f32 = jnp.float32

    def key_copy(stage):
        size = 1 << (len(bits) - 1 - stage)
        return pltpu.make_async_remote_copy(
            src_ref=(acc if stage else keyed).at[pl.ds(size, size)],
            dst_ref=taken.at[pl.ds(size, size)],
            send_sem=key_send.at[stage],
            recv_sem=key_recv.at[stage],
            device_id={"row": row_partner(bits[stage])},
            device_id_type=MESH,
        )

    def key_add(stage):
        size = 1 << (len(bits) - 1 - stage)
        key_copy(stage).wait_recv()
        for index in range(size):
            block = keyed[index] if stage == 0 else acc[index]
            both = block.astype(f32) + taken[size + index].astype(f32)
            if stage == len(bits) - 1:
                key_total[...] = both.astype(key_total.dtype)
            else:
                acc[index] = both.astype(acc.dtype)

    if bits:
        key_copy(0).start()

    def extra_copy(step):
        return pltpu.make_async_remote_copy(
            src_ref=extra,
            dst_ref=extras.at[me],
            send_sem=extra_send.at[step],
            recv_sem=extra_recv.at[step],
            device_id={"head": lax.rem(me + step, n)},
            device_id_type=MESH,
        )

    if small:
        for step in range(1, n):
            extra_copy(step).start()
        extra_own = pltpu.make_async_copy(extra, extras.at[me], extra_local)
        extra_own.start()

    def copy_of(side, block):
        return pltpu.make_async_remote_copy(
            src_ref=sends.at[side, block],
            dst_ref=recvs.at[side, block],
            send_sem=send.at[side, block],
            recv_sem=recv.at[side, block],
            device_id={"head": me + (1 if side == 0 else -1)},
            device_id_type=MESH,
        )

    def pass_on(side, block, inner):
        copy = copy_of(side, block)

        @pl.when(inner)
        def _():
            copy.wait_recv()
            sends[side, block] = (
                x[block].astype(f32) + recvs[side, block].astype(f32)
            ).astype(sends.dtype)

        @pl.when(jnp.logical_not(inner))
        def _():
            sends[side, block] = x[block]

        copy.start()

    for step in range(n - 1):
        high, low = n - 1 - step, step
        pl.when(me < high)(lambda: pass_on(0, high, me > 0))
        pl.when(me > low)(lambda: pass_on(1, low, me < n - 1))
        if step == 0:
            for stage in range(len(bits) - 1):
                key_add(stage)
                key_copy(stage + 1).start()

    total[...] = x[me].astype(f32)

    @pl.when(me > 0)
    def _():
        copy_of(0, me).wait_recv()
        total[...] += recvs[0, me].astype(f32)

    @pl.when(me < n - 1)
    def _():
        copy_of(1, me).wait_recv()
        total[...] += recvs[1, me].astype(f32)

    for step in range(n - 1):
        high, low = n - 1 - step, step
        pl.when(me < high)(lambda: copy_of(0, high).wait_send())
        pl.when(me > low)(lambda: copy_of(1, low).wait_send())
    if bits:
        key_add(len(bits) - 1)
        for stage in range(len(bits)):
            key_copy(stage).wait_send()
    if small:
        for step in range(1, n):
            origin = lax.rem(me + n - step, n)
            extra_copy(step).wait_send()
            pltpu.make_async_remote_copy(
                src_ref=extra,
                dst_ref=extras.at[origin],
                send_sem=extra_send.at[step],
                recv_sem=extra_recv.at[step],
                device_id={"head": origin},
                device_id_type=MESH,
            ).wait_recv()
        extra_own.wait()


def line_sum(number, name, x, extra=None, keyed=None):
    n, block = x.shape[0], x.shape[1:]
    small = extra is not None
    bits = row_bits()[::-1] if keyed is not None else []
    arrays = [x] + [array for array in (extra, keyed) if array is not None]
    shapes = [jax.ShapeDtypeStruct(block, jnp.float32)]
    scratch = [
        pltpu.VMEM((2,) + x.shape, x.dtype),
        pltpu.VMEM((2,) + x.shape, x.dtype),
        pltpu.SemaphoreType.DMA((2, n)),
        pltpu.SemaphoreType.DMA((2, n)),
    ]
    if small:
        shapes.append(jax.ShapeDtypeStruct((n,) + extra.shape, extra.dtype))
        scratch += [
            pltpu.SemaphoreType.DMA((n,)),
            pltpu.SemaphoreType.DMA((n,)),
            pltpu.SemaphoreType.DMA,
        ]
    if bits:
        shapes.append(jax.ShapeDtypeStruct(keyed.shape[1:], keyed.dtype))
        scratch += [
            pltpu.VMEM(keyed.shape, keyed.dtype),
            pltpu.VMEM(keyed.shape, keyed.dtype),
            pltpu.SemaphoreType.DMA((len(bits),)),
            pltpu.SemaphoreType.DMA((len(bits),)),
        ]
    return pl.pallas_call(
        functools.partial(line_sum_kernel, n, small, tuple(bits)),
        out_shape=shapes,
        in_specs=[pl.BlockSpec(memory_space=pltpu.VMEM)] * len(arrays),
        out_specs=[pl.BlockSpec(memory_space=pltpu.VMEM)] * len(shapes),
        scratch_shapes=scratch,
        compiler_params=pltpu.CompilerParams(
            collective_id=number, has_side_effects=True, vmem_limit_bytes=40 * 1024 * 1024
        ),
        cost_estimate=pl.CostEstimate(
            flops=0, bytes_accessed=50 * x.size * x.dtype.itemsize, transcendentals=0
        ),
        name=name,
    )(*arrays)


def attention_kernel(q_ref, k_ref, v_ref, g_ref, o_ref, dq_ref, dkv_ref):
    scaling = HD ** (-0.5)
    query, cot = q_ref[...], g_ref[...]
    keys = k_ref[...].reshape(-1, HD)
    values = v_ref[...].reshape(-1, HD)
    last = (((1,), (1,)), ((), ()))
    first = (((0,), (0,)), ((), ()))
    scores = lax.dot_general(query, keys, last, preferred_element_type=jnp.float32) * scaling
    top = jnp.max(scores, axis=-1, keepdims=True)
    weights = jnp.exp(scores - top)
    inverse = 1.0 / jnp.sum(weights, axis=-1, keepdims=True)
    out = jnp.dot(weights.astype(jnp.bfloat16), values, preferred_element_type=jnp.float32)
    out = (out * inverse).astype(jnp.bfloat16)
    o_ref[...] = out
    dsum = jnp.sum(cot.astype(jnp.float32) * out.astype(jnp.float32), axis=-1, keepdims=True)
    probs = weights * inverse
    dprobs = lax.dot_general(cot, values, last, preferred_element_type=jnp.float32)
    dscores = (probs * (dprobs - dsum)).astype(jnp.bfloat16)
    dquery = jnp.dot(dscores, keys, preferred_element_type=jnp.float32) * scaling
    dq_ref[...] = dquery.astype(jnp.bfloat16)
    dkey = lax.dot_general(dscores, query, first, preferred_element_type=jnp.float32) * scaling
    rows, unused, tok, unused = dkv_ref.shape
    dkv_ref[:, 0] = dkey.astype(jnp.bfloat16).reshape(rows, tok, HD)
    dval = lax.dot_general(
        probs.astype(jnp.bfloat16), cot, first, preferred_element_type=jnp.float32
    )
    dkv_ref[:, 1] = dval.astype(jnp.bfloat16).reshape(rows, tok, HD)


def attention(query, keys, values, cot):
    tok, width = query.shape
    rows = keys.shape[0]
    own = pl.BlockSpec((tok, HD), lambda h: (0, h))
    every = pl.BlockSpec((rows, tok, HD), lambda h: (0, 0, h))
    small = jax.ShapeDtypeStruct((tok, width), jnp.bfloat16)
    large = jax.ShapeDtypeStruct((rows, 2, tok, width), jnp.bfloat16)
    pair = pl.BlockSpec((rows, 2, tok, HD), lambda h: (0, 0, 0, h))
    return pl.pallas_call(
        attention_kernel,
        grid=(width // HD,),
        out_shape=[small, small, large],
        in_specs=[own, every, every, own],
        out_specs=[own, own, pair],
        compiler_params=pltpu.CompilerParams(vmem_limit_bytes=50 * 1024 * 1024),
        name="attention",
    )(query, keys, values, cot)


def dot(a, b, dims):
    return lax.dot_general(a, b, (dims, ((), ())), preferred_element_type=jnp.float32)


def row_bits():
    bits, bit = [], lax.axis_size("row") // 2
    while bit:
        bits.append(bit)
        bit //= 2
    return bits


def row_swap(x, bit):
    return lax.ppermute(x, "row", [(row, row ^ bit) for row in range(lax.axis_size("row"))])


def cube_gather(x, dim):
    for bit in row_bits():
        x = jnp.concatenate([x, row_swap(x, bit)], axis=dim)
    return x


def cube_deal(x):
    row = lax.axis_index("row")
    for bit in row_bits():
        cols = x.shape[1] // 2
        upper = (row // bit) % 2 == 1
        low, high = x[:, :cols], x[:, cols:]
        kept, sent = jnp.where(upper, high, low), jnp.where(upper, low, high)
        x = jnp.concatenate([kept, row_swap(sent, bit)], axis=0)
    return x


def on_device(latent, hint, timestep, modulation, qkv_weight, out_weight, zero_weight, cotangent):
    f32, bf16 = jnp.float32, jnp.bfloat16
    tok, width = latent.shape
    half = tok // 2
    n_head, n_row = lax.axis_size("head"), lax.axis_size("row")
    full_width = n_head * width
    group_pos = lax.axis_index("group")
    control = group_pos == 0
    head_pos = lax.axis_index("head")
    steps_count = modulation.shape[1]
    pick = (lax.broadcasted_iota(jnp.int32, (steps_count,), 0) == timestep[0]).astype(f32)
    mods = jnp.sum(modulation[0] * pick[:, None, None], axis=0)
    shift, scale, gate = (mods[0], mods[1], mods[2])
    gate_dev = lax.dynamic_slice_in_dim(gate, head_pos * width, width, 0)
    scale_dev = lax.dynamic_slice_in_dim(scale, head_pos * width, width, 0)
    w_qkv, w_out = qkv_weight[0], out_weight[0]

    def widen(blocks):
        return jnp.concatenate([blocks[index] for index in range(n_head)], axis=1)

    def swap(x):
        return lax.ppermute(x, "group", [(0, 1), (1, 0)])

    def near(x):
        return jnp.where(control, x, lax.ppermute(x, "group", [(0, 1)]))

    def near_cols(x):
        cols = x.shape[1] // 2
        return jnp.where(control, x[:, :cols], lax.ppermute(x[:, cols:], "group", [(0, 1)]))

    def head_terms(x, weight):
        return jnp.stack(
            [
                dot(x, weight[index * width : (index + 1) * width], ((1,), (1,))).astype(bf16)
                for index in range(n_head)
            ]
        )

    summed = (latent.astype(f32) + hint.astype(f32)).astype(bf16)
    inputs = jnp.where(control, summed, latent)
    cot_own = jnp.where(control, cotangent[:half], cotangent[half:])
    cot_half, whole = line_gather(0, "gather_inputs", (cot_own, None), (inputs, None))
    cot_half = widen(cot_half)
    hint_half = dot(cot_half, zero_weight, ((1,), (0,))).astype(bf16)
    hint_other = swap(hint_half)
    cot_other = swap(cot_half)

    whole_f = widen(whole).astype(f32)
    mean = jnp.mean(whole_f, axis=-1, keepdims=True)
    centred = whole_f - mean
    var = jnp.mean(centred * centred, axis=-1, keepdims=True)
    rstd = lax.rsqrt(var + EPS)
    nhat = centred * rstd
    normed = (nhat * (1.0 + scale) + shift).astype(bf16)
    keys, values, query = [
        dot(normed, w_qkv[index], ((1,), (0,))).astype(bf16) for index in (1, 2, 0)
    ]
    all_keys = cube_gather(keys[None], 0)
    all_values = cube_gather(values[None], 0)

    hint_back = jnp.concatenate([hint_half, hint_other])
    incoming = jnp.where(control, hint_back, cotangent)
    gated = (gate_dev * hint_back.astype(f32)).astype(bf16)
    (gated_blocks,) = line_gather(1, "gather_gated", (gated, 0))
    cot_full = jnp.where(
        control,
        jnp.concatenate([cot_half, cot_other]),
        jnp.concatenate([cot_other, cot_half]),
    )
    gated_main = (gate * cot_full.astype(f32)).astype(bf16)
    gated_full = lax.optimization_barrier(
        jnp.where(control, widen(gated_blocks), gated_main)
    )
    attn_grad = dot(gated_full, w_out, ((1,), (0,))).astype(bf16)
    attn, dquery, key_terms = attention(query, all_keys, all_values, attn_grad)

    branch, dkv = line_sum(2, "sum_branch", head_terms(attn, w_out), keyed=key_terms)
    state = (inputs.astype(f32) + gate_dev * branch).astype(bf16)
    near_state = near(state)
    dkey, dval = dkv[0], dkv[1]
    grads = [dquery, dkey, dval]

    scaled_nhat = nhat * (1.0 + scale)
    terms = []
    first, second = 0.0, 0.0
    for index in range(n_head):
        cols = slice(index * width, (index + 1) * width)
        term = sum(dot(grads[c], w_qkv[c, cols], ((1,), (1,))) for c in range(3))
        first = first + jnp.sum(term * (1.0 + scale[cols]), axis=-1)
        second = second + jnp.sum(term * scaled_nhat[:, cols], axis=-1)
        terms.append(term.astype(bf16))
    sums = jnp.concatenate([first[None], second[None], jnp.zeros((6, tok), f32)])
    state_half = jnp.where(control, near_state[:half], near_state[half:])
    hint_terms = head_terms(state_half, zero_weight)
    near_attn, near_query, near_gated = near(attn), near(dquery), near_cols(gated_full)
    terms, hint_terms, near_attn, near_query, near_gated = lax.optimization_barrier(
        (terms, hint_terms, near_attn, near_query, near_gated)
    )
    both = jnp.concatenate([jnp.stack(terms), hint_terms], axis=1)
    both, sum_parts = line_sum(3, "sum_norm_hint", both, sums)
    dnorm, projected = both[:tok], both[tok:]
    sums = jnp.sum(sum_parts, axis=0) / full_width
    nhat_dev = lax.dynamic_slice_in_dim(nhat, head_pos * width, width, 1)
    scaled = dnorm * (1.0 + scale_dev)
    d_in = incoming.astype(f32) + rstd * (
        scaled - sums[0][:, None] - nhat_dev * sums[1][:, None]
    )
    own_half = jnp.where(control, d_in[:half], d_in[half:])
    sent_half = jnp.where(control, d_in[half:], d_in[:half])
    other_half = swap(sent_half.astype(bf16)).astype(f32)
    latent_grad = (own_half + other_half)[None, None]
    hint_grad = jnp.where(control, own_half, other_half)[None, None]

    main_state = lax.ppermute(state[:half], "group", [(1, 0)])
    main_half = jnp.where(control, main_state, state[half:])
    mixed_half = (main_half.astype(f32) + projected).astype(bf16)
    mixed_other = swap(mixed_half)
    mixed = jnp.where(
        control,
        jnp.concatenate([mixed_half, mixed_other]),
        jnp.concatenate([mixed_other, mixed_half]),
    )

    tokens = ((0,), (0,))
    normed_cols = cube_deal(near_cols(normed))
    near_grads = [near_query, near(dkey), near(dval)]
    qkv_grad = jnp.stack(
        [dot(normed_cols, cube_gather(x, 0), tokens) for x in near_grads], axis=1
    )
    out_grad = dot(cube_deal(near_gated), cube_gather(near_attn, 0), tokens)
    cot_cols = jnp.where(
        control, cot_full[:, : full_width // 2], cot_full[:, full_width // 2 :]
    )
    zero_grad = dot(cube_deal(cot_cols), cube_gather(near_state, 0), tokens)
    return (mixed, latent_grad, hint_grad, qkv_grad, out_grad, zero_grad)


def solution(mesh):
    placed = (
        P("row", "head"),
        P("row", "head"),
        P(),
        P("group", None, None, None),
        P("group", None, None, "head"),
        P("group", None, "head"),
        P(None, "head"),
        P("row", "head"),
    )
    return jax.shard_map(
        on_device,
        mesh=mesh,
        in_specs=placed,
        out_specs=(
            P("row", "head"),
            P("row", "group", None, "head"),
            P("row", "group", None, "head"),
            P(("group", "row"), None, "head"),
            P(("group", "row"), "head"),
            P(("group", "row"), "head"),
        ),
        check_vma=False,
    )
```

```python
import functools

import jax
import jax.numpy as jnp
from jax import lax
from jax.experimental import pallas as pl
from jax.experimental.pallas import tpu as pltpu
from jax.sharding import PartitionSpec as P

HD = 128


EPS = 1e-06

MESH = pl.DeviceIdType.MESH


def greet(peers, row_peers=()):
    barrier = pltpu.get_barrier_semaphore()
    for peer in peers:
        pl.semaphore_signal(barrier, inc=1, device_id={"head": peer}, device_id_type=MESH)
    for peer in row_peers:
        pl.semaphore_signal(barrier, inc=1, device_id={"row": peer}, device_id_type=MESH)
    pl.semaphore_wait(barrier, len(peers) + len(row_peers))


def row_partner(bit):
    row = lax.axis_index("row")
    return row + bit - 2 * bit * ((row // bit) % 2)


def others(me, n):
    return [lax.rem(me + step, n) for step in range(1, n)]


def line_gather_kernel(n, sources, *refs):
    count = len(sources)
    ins, outs, sems = refs[:count], refs[count : 2 * count], refs[2 * count :]
    me = lax.axis_index("head")
    greet(others(me, n))
    group = lax.axis_index("group")

    def part(number, block):
        width = ins[number].shape[1]
        return outs[number].at[:, pl.ds(pl.multiple_of(block * width, 128), width)]

    def copy_of(number, block, way):
        send, recv = sems[3 * number : 3 * number + 2]
        side = 0 if way > 0 else 1
        return pltpu.make_async_remote_copy(
            src_ref=part(number, block),
            dst_ref=part(number, block),
            send_sem=send.at[side, block],
            recv_sem=recv.at[side, block],
            device_id={"head": me + way},
            device_id_type=MESH,
        )

    def own_copy(number, way):
        send, recv = sems[3 * number : 3 * number + 2]
        side = 0 if way > 0 else 1
        return pltpu.make_async_remote_copy(
            src_ref=ins[number],
            dst_ref=part(number, me),
            send_sem=send.at[side, me],
            recv_sem=recv.at[side, me],
            device_id={"head": me + way},
            device_id_type=MESH,
        )

    def active(number, work):
        source = sources[number]
        if source is None:
            work()
        else:
            pl.when(group == source)(work)

    def local_copy(number):
        return pltpu.make_async_copy(ins[number], part(number, me), sems[3 * number + 2])

    def begin(number):
        pl.when(me < n - 1)(lambda: own_copy(number, 1).start())
        pl.when(me > 0)(lambda: own_copy(number, -1).start())
        local_copy(number).start()

    def hop(number, distance):
        @pl.when(me >= distance)
        def _():
            copy = copy_of(number, me - distance, 1)
            copy.wait_recv()
            pl.when(me < n - 1)(copy.start)

        @pl.when(me + distance < n)
        def _():
            copy = copy_of(number, me + distance, -1)
            copy.wait_recv()
            pl.when(me > 0)(copy.start)

    def finish(number):
        for distance in range(n):
            @pl.when((me >= distance) & (me < n - 1))
            def _():
                copy_of(number, me - distance, 1).wait_send()

            @pl.when((me + distance < n) & (me > 0))
            def _():
                copy_of(number, me + distance, -1).wait_send()
        local_copy(number).wait()

    for number in range(count):
        active(number, functools.partial(begin, number))
    for distance in range(1, n):
        for number in range(count):
            active(number, functools.partial(hop, number, distance))
    for number in range(count):
        active(number, functools.partial(finish, number))


def line_gather(number, name, *wants):
    n = lax.axis_size("head")
    scratch = []
    for x, source in wants:
        scratch += [
            pltpu.SemaphoreType.DMA((2, n)),
            pltpu.SemaphoreType.DMA((2, n)),
            pltpu.SemaphoreType.DMA,
        ]
    arrays = [x for x, source in wants]
    sent = sum(x.size * x.dtype.itemsize for x in arrays)
    return pl.pallas_call(
        functools.partial(line_gather_kernel, n, tuple(source for x, source in wants)),
        out_shape=[jax.ShapeDtypeStruct((x.shape[0], n * x.shape[1]), x.dtype) for x in arrays],
        in_specs=[pl.BlockSpec(memory_space=pl.ANY)] * len(arrays),
        out_specs=[pl.BlockSpec(memory_space=pl.ANY)] * len(arrays),
        scratch_shapes=scratch,
        compiler_params=pltpu.CompilerParams(collective_id=number, has_side_effects=True),
        cost_estimate=pl.CostEstimate(flops=0, bytes_accessed=200 * sent, transcendentals=0),
        name=name,
    )(*arrays)


def line_sum_kernel(n, small, bits, *refs):
    if bits:
        x, keyed, total, key_total, *scratch = refs
        acc, taken, key_send, key_recv = scratch[-4:]
    elif small:
        x, extra, total, extras, *scratch = refs
        extra_send, extra_recv, extra_local = scratch[-3:]
    else:
        x, total, *scratch = refs
    sends, recvs, send, recv = scratch[:4]
    me = lax.axis_index("head")
    greet(others(me, n), [row_partner(bit) for bit in bits])
    f32 = jnp.float32
    width = total.shape[1]

    def key_copy(stage):
        size = 1 << (len(bits) - 1 - stage)
        return pltpu.make_async_remote_copy(
            src_ref=(acc if stage else keyed).at[pl.ds(size, size)],
            dst_ref=taken.at[pl.ds(size, size)],
            send_sem=key_send.at[stage],
            recv_sem=key_recv.at[stage],
            device_id={"row": row_partner(bits[stage])},
            device_id_type=MESH,
        )

    def key_add(stage):
        size = 1 << (len(bits) - 1 - stage)
        key_copy(stage).wait_recv()
        for index in range(size):
            block = keyed[index] if stage == 0 else acc[index]
            both = block.astype(f32) + taken[size + index].astype(f32)
            if stage == len(bits) - 1:
                key_total[...] = both.astype(key_total.dtype)
            else:
                acc[index] = both.astype(acc.dtype)

    if bits:
        key_copy(0).start()

    def extra_copy(step):
        return pltpu.make_async_remote_copy(
            src_ref=extra,
            dst_ref=extras.at[me],
            send_sem=extra_send.at[step],
            recv_sem=extra_recv.at[step],
            device_id={"head": lax.rem(me + step, n)},
            device_id_type=MESH,
        )

    if small:
        for step in range(1, n):
            extra_copy(step).start()
        extra_own = pltpu.make_async_copy(extra, extras.at[me], extra_local)
        extra_own.start()

    def part(block):
        return x[:, pl.ds(pl.multiple_of(block * width, 128), width)]

    def copy_of(side, block):
        return pltpu.make_async_remote_copy(
            src_ref=sends.at[side, block],
            dst_ref=recvs.at[side, block],
            send_sem=send.at[side, block],
            recv_sem=recv.at[side, block],
            device_id={"head": me + (1 if side == 0 else -1)},
            device_id_type=MESH,
        )

    def pass_on(side, block, inner):
        copy = copy_of(side, block)

        @pl.when(inner)
        def _():
            copy.wait_recv()
            sends[side, block] = (
                part(block).astype(f32) + recvs[side, block].astype(f32)
            ).astype(sends.dtype)

        @pl.when(jnp.logical_not(inner))
        def _():
            sends[side, block] = part(block)

        copy.start()

    for step in range(n - 1):
        high, low = n - 1 + me - step, step + me - (n - 1)
        pl.when(me <= step)(functools.partial(pass_on, 0, high, me > 0))
        pl.when(low >= 0)(functools.partial(pass_on, 1, low, me < n - 1))
        if step == 0:
            for stage in range(len(bits) - 1):
                key_add(stage)
                key_copy(stage + 1).start()

    total[...] = part(me).astype(f32)

    @pl.when(me > 0)
    def _():
        copy_of(0, me).wait_recv()
        total[...] += recvs[0, me].astype(f32)

    @pl.when(me < n - 1)
    def _():
        copy_of(1, me).wait_recv()
        total[...] += recvs[1, me].astype(f32)

    for step in range(n - 1):
        high, low = n - 1 - step, step
        pl.when(me < high)(lambda: copy_of(0, high).wait_send())
        pl.when(me > low)(lambda: copy_of(1, low).wait_send())
    if bits:
        key_add(len(bits) - 1)
        for stage in range(len(bits)):
            key_copy(stage).wait_send()
    if small:
        for step in range(1, n):
            origin = lax.rem(me + n - step, n)
            extra_copy(step).wait_send()
            pltpu.make_async_remote_copy(
                src_ref=extra,
                dst_ref=extras.at[origin],
                send_sem=extra_send.at[step],
                recv_sem=extra_recv.at[step],
                device_id={"head": origin},
                device_id_type=MESH,
            ).wait_recv()
        extra_own.wait()


def line_sum(number, name, x, extra=None, keyed=None):
    n = lax.axis_size("head")
    block = (x.shape[0], x.shape[1] // n)
    small = extra is not None
    bits = row_bits()[::-1] if keyed is not None else []
    arrays = [x] + [array for array in (extra, keyed) if array is not None]
    shapes = [jax.ShapeDtypeStruct(block, jnp.float32)]
    scratch = [
        pltpu.VMEM((2, n) + block, x.dtype),
        pltpu.VMEM((2, n) + block, x.dtype),
        pltpu.SemaphoreType.DMA((2, n)),
        pltpu.SemaphoreType.DMA((2, n)),
    ]
    if small:
        shapes.append(jax.ShapeDtypeStruct((n,) + extra.shape, extra.dtype))
        scratch += [
            pltpu.SemaphoreType.DMA((n,)),
            pltpu.SemaphoreType.DMA((n,)),
            pltpu.SemaphoreType.DMA,
        ]
    if bits:
        shapes.append(jax.ShapeDtypeStruct(keyed.shape[1:], keyed.dtype))
        scratch += [
            pltpu.VMEM(keyed.shape, keyed.dtype),
            pltpu.VMEM(keyed.shape, keyed.dtype),
            pltpu.SemaphoreType.DMA((len(bits),)),
            pltpu.SemaphoreType.DMA((len(bits),)),
        ]
    return pl.pallas_call(
        functools.partial(line_sum_kernel, n, small, tuple(bits)),
        out_shape=shapes,
        in_specs=[pl.BlockSpec(memory_space=pltpu.VMEM)] * len(arrays),
        out_specs=[pl.BlockSpec(memory_space=pltpu.VMEM)] * len(shapes),
        scratch_shapes=scratch,
        compiler_params=pltpu.CompilerParams(
            collective_id=number, has_side_effects=True, vmem_limit_bytes=40 * 1024 * 1024
        ),
        cost_estimate=pl.CostEstimate(
            flops=0, bytes_accessed=50 * x.size * x.dtype.itemsize, transcendentals=0
        ),
        name=name,
    )(*arrays)


def attention_kernel(q_ref, k_ref, v_ref, g_ref, o_ref, dq_ref, dkv_ref):
    scaling = HD ** (-0.5)
    query, cot = q_ref[...], g_ref[...]
    keys = k_ref[...].reshape(-1, HD)
    values = v_ref[...].reshape(-1, HD)
    last = (((1,), (1,)), ((), ()))
    first = (((0,), (0,)), ((), ()))
    scores = lax.dot_general(query, keys, last, preferred_element_type=jnp.float32) * scaling
    top = jnp.max(scores, axis=-1, keepdims=True)
    weights = jnp.exp(scores - top)
    inverse = 1.0 / jnp.sum(weights, axis=-1, keepdims=True)
    out = jnp.dot(weights.astype(jnp.bfloat16), values, preferred_element_type=jnp.float32)
    out = (out * inverse).astype(jnp.bfloat16)
    o_ref[...] = out
    dsum = jnp.sum(cot.astype(jnp.float32) * out.astype(jnp.float32), axis=-1, keepdims=True)
    probs = weights * inverse
    dprobs = lax.dot_general(cot, values, last, preferred_element_type=jnp.float32)
    dscores = (probs * (dprobs - dsum)).astype(jnp.bfloat16)
    dquery = jnp.dot(dscores, keys, preferred_element_type=jnp.float32) * scaling
    dq_ref[...] = dquery.astype(jnp.bfloat16)
    dkey = lax.dot_general(dscores, query, first, preferred_element_type=jnp.float32) * scaling
    rows, unused, tok, unused = dkv_ref.shape
    dkv_ref[:, 0] = dkey.astype(jnp.bfloat16).reshape(rows, tok, HD)
    dval = lax.dot_general(
        probs.astype(jnp.bfloat16), cot, first, preferred_element_type=jnp.float32
    )
    dkv_ref[:, 1] = dval.astype(jnp.bfloat16).reshape(rows, tok, HD)


def attention(query, keys, values, cot):
    tok, width = query.shape
    rows = keys.shape[0]
    own = pl.BlockSpec((tok, HD), lambda h: (0, h))
    every = pl.BlockSpec((rows, tok, HD), lambda h: (0, 0, h))
    small = jax.ShapeDtypeStruct((tok, width), jnp.bfloat16)
    large = jax.ShapeDtypeStruct((rows, 2, tok, width), jnp.bfloat16)
    pair = pl.BlockSpec((rows, 2, tok, HD), lambda h: (0, 0, 0, h))
    return pl.pallas_call(
        attention_kernel,
        grid=(width // HD,),
        out_shape=[small, small, large],
        in_specs=[own, every, every, own],
        out_specs=[own, own, pair],
        compiler_params=pltpu.CompilerParams(vmem_limit_bytes=50 * 1024 * 1024),
        name="attention",
    )(query, keys, values, cot)


def dot(a, b, dims):
    return lax.dot_general(a, b, (dims, ((), ())), preferred_element_type=jnp.float32)


def row_bits():
    bits, bit = [], lax.axis_size("row") // 2
    while bit:
        bits.append(bit)
        bit //= 2
    return bits


def row_swap(x, bit):
    return lax.ppermute(x, "row", [(row, row ^ bit) for row in range(lax.axis_size("row"))])


def cube_gather(x, dim):
    for bit in row_bits():
        x = jnp.concatenate([x, row_swap(x, bit)], axis=dim)
    return x


def cube_deal(x):
    row = lax.axis_index("row")
    for bit in row_bits():
        cols = x.shape[1] // 2
        upper = (row // bit) % 2 == 1
        low, high = x[:, :cols], x[:, cols:]
        kept, sent = jnp.where(upper, high, low), jnp.where(upper, low, high)
        x = jnp.concatenate([kept, row_swap(sent, bit)], axis=0)
    return x


def on_device(latent, hint, timestep, modulation, qkv_weight, out_weight, zero_weight, cotangent):
    f32, bf16 = jnp.float32, jnp.bfloat16
    tok, width = latent.shape
    half = tok // 2
    n_head, n_row = lax.axis_size("head"), lax.axis_size("row")
    full_width = n_head * width
    group_pos = lax.axis_index("group")
    control = group_pos == 0
    head_pos = lax.axis_index("head")
    steps_count = modulation.shape[1]
    pick = (lax.broadcasted_iota(jnp.int32, (steps_count,), 0) == timestep[0]).astype(f32)
    mods = jnp.sum(modulation[0] * pick[:, None, None], axis=0)
    shift, scale, gate = (mods[0], mods[1], mods[2])
    gate_dev = lax.dynamic_slice_in_dim(gate, head_pos * width, width, 0)
    scale_dev = lax.dynamic_slice_in_dim(scale, head_pos * width, width, 0)
    w_qkv, w_out = qkv_weight[0], out_weight[0]

    def swap(x):
        return lax.ppermute(x, "group", [(0, 1), (1, 0)])

    def near(x):
        return jnp.where(control, x, lax.ppermute(x, "group", [(0, 1)]))

    def near_cols(x):
        cols = x.shape[1] // 2
        return jnp.where(control, x[:, :cols], lax.ppermute(x[:, cols:], "group", [(0, 1)]))

    def head_terms(x, weight):
        return dot(x, weight, ((1,), (1,))).astype(bf16)

    summed = (latent.astype(f32) + hint.astype(f32)).astype(bf16)
    inputs = jnp.where(control, summed, latent)
    cot_own = jnp.where(control, cotangent[:half], cotangent[half:])
    cot_half, whole = line_gather(0, "gather_inputs", (cot_own, None), (inputs, None))
    hint_half = dot(cot_half, zero_weight, ((1,), (0,))).astype(bf16)
    hint_other = swap(hint_half)
    cot_other = swap(cot_half)

    whole_f = whole.astype(f32)
    mean = jnp.mean(whole_f, axis=-1, keepdims=True)
    centred = whole_f - mean
    var = jnp.mean(centred * centred, axis=-1, keepdims=True)
    rstd = lax.rsqrt(var + EPS)
    nhat = centred * rstd
    normed = (nhat * (1.0 + scale) + shift).astype(bf16)
    keys, values, query = [
        dot(normed, w_qkv[index], ((1,), (0,))).astype(bf16) for index in (1, 2, 0)
    ]
    all_keys = cube_gather(keys[None], 0)
    all_values = cube_gather(values[None], 0)

    hint_back = jnp.concatenate([hint_half, hint_other])
    incoming = jnp.where(control, hint_back, cotangent)
    gated = (gate_dev * hint_back.astype(f32)).astype(bf16)
    (gated_full,) = line_gather(1, "gather_gated", (gated, 0))
    cot_full = jnp.concatenate(
        [jnp.where(control, cot_half, cot_other), jnp.where(control, cot_other, cot_half)]
    )
    cot_full = lax.optimization_barrier(cot_full)
    gated_main = (gate * cot_full.astype(f32)).astype(bf16)
    gated_full = lax.optimization_barrier(
        jnp.where(control, gated_full, gated_main)
    )
    attn_grad = dot(gated_full, w_out, ((1,), (0,))).astype(bf16)
    attn, dquery, key_terms = attention(query, all_keys, all_values, attn_grad)

    branch, dkv = line_sum(2, "sum_branch", head_terms(attn, w_out), keyed=key_terms)
    state = (inputs.astype(f32) + gate_dev * branch).astype(bf16)
    near_state = near(state)
    dkey, dval = dkv[0], dkv[1]
    grads = [dquery, dkey, dval]

    terms = sum(dot(grads[c], w_qkv[c], ((1,), (1,))) for c in range(3))
    terms = lax.optimization_barrier(terms)
    scaled_terms = terms * (1.0 + scale)
    first = jnp.sum(scaled_terms, axis=-1)
    second = jnp.sum(scaled_terms * nhat, axis=-1)
    terms = terms.astype(bf16)
    sums = jnp.concatenate([first[None], second[None], jnp.zeros((6, tok), f32)])
    state_half = jnp.where(control, near_state[:half], near_state[half:])
    hint_terms = head_terms(state_half, zero_weight)
    near_attn, near_query, near_gated = near(attn), near(dquery), near_cols(gated_full)
    terms, hint_terms, near_attn, near_query, near_gated = lax.optimization_barrier(
        (terms, hint_terms, near_attn, near_query, near_gated)
    )
    both = jnp.concatenate([terms, hint_terms])
    both, sum_parts = line_sum(3, "sum_norm_hint", both, sums)
    dnorm, projected = both[:tok], both[tok:]
    sums = jnp.sum(sum_parts, axis=0) / full_width
    nhat_dev = lax.dynamic_slice_in_dim(nhat, head_pos * width, width, 1)
    scaled = dnorm * (1.0 + scale_dev)
    d_in = incoming.astype(f32) + rstd * (
        scaled - sums[0][:, None] - nhat_dev * sums[1][:, None]
    )
    own_half = jnp.where(control, d_in[:half], d_in[half:])
    sent_half = jnp.where(control, d_in[half:], d_in[:half])
    other_half = swap(sent_half.astype(bf16)).astype(f32)
    latent_grad = (own_half + other_half)[None, None]
    hint_grad = jnp.where(control, own_half, other_half)[None, None]

    main_state = lax.ppermute(state[:half], "group", [(1, 0)])
    main_half = jnp.where(control, main_state, state[half:])
    mixed_half = (main_half.astype(f32) + projected).astype(bf16)
    mixed_other = swap(mixed_half)
    mixed = jnp.where(
        control,
        jnp.concatenate([mixed_half, mixed_other]),
        jnp.concatenate([mixed_other, mixed_half]),
    )

    tokens = ((0,), (0,))
    normed_cols = cube_deal(near_cols(normed))
    near_grads = [near_query, near(dkey), near(dval)]
    qkv_grad = jnp.stack(
        [dot(normed_cols, cube_gather(x, 0), tokens) for x in near_grads], axis=1
    )
    out_grad = dot(cube_deal(near_gated), cube_gather(near_attn, 0), tokens)
    cot_cols = jnp.where(
        control, cot_full[:, : full_width // 2], cot_full[:, full_width // 2 :]
    )
    zero_grad = dot(cube_deal(cot_cols), cube_gather(near_state, 0), tokens)
    return (mixed, latent_grad, hint_grad, qkv_grad, out_grad, zero_grad)


def solution(mesh):
    placed = (
        P("row", "head"),
        P("row", "head"),
        P(),
        P("group", None, None, None),
        P("group", None, None, "head"),
        P("group", None, "head"),
        P(None, "head"),
        P("row", "head"),
    )
    return jax.shard_map(
        on_device,
        mesh=mesh,
        in_specs=placed,
        out_specs=(
            P("row", "head"),
            P("row", "group", None, "head"),
            P("row", "group", None, "head"),
            P(("group", "row"), None, "head"),
            P(("group", "row"), "head"),
            P(("group", "row"), "head"),
        ),
        check_vma=False,
    )
```
